32 devices in a mesh: parts: 2 (over x), ex: 16 (over z, y, core).
Axes of the slice: x: 2, y: 2, z: 4, core: 2. Of those that a mesh axis runs over, the one named last changes fastest.
Arguments:
- train_grads: float32 [2, 32768, 1024], P(None, ('parts', 'ex')), parts along dimension 1, may hold values from -300 to 300
- query_grads: float32 [2, 256, 1024], P(None, ('parts', 'ex')), parts along dimension 1, may hold values from -6 to 6
Outputs:
- scores: float32 [128, 32768], P(None, ('parts', 'ex')), parts along dimension 1
The draws below stay inside these ranges and needn't reach their ends.
There are 2 independent parts, one for each index of `parts`. The reference program is written for one: setup_inputs(seed, part) draws one part's arguments, and reference() takes and returns one part's arrays. A program takes and returns all parts, laid end to end along the dimension named above; each array names one. Nothing has to cross between parts.
All inputs are finite; a program needn't handle non-finite values.
Results may differ from the reference program's by a relative error of at most 0.0003.
Values sent between devices are 32-bit elements; how exact they have to be, the bound alone decides.
A program may use at most 128 MiB of HBM per device.

```python
import math
import jax
import jax.numpy as jnp
from jax import lax

K = 1024
L = 2
ITERS = 12
NTRAIN = 16384
NQ = 128


def draw_train_grads(key, part):
    first, second, third = jax.random.split(key, 3)
    base = jnp.clip(jax.random.normal(first, (L, NTRAIN, K), jnp.float32), -6.0, 6.0)
    columns = jnp.exp(jax.random.uniform(second, (L, 1, K), jnp.float32) * math.log(10.0))
    rows_scale = jnp.exp(jax.random.uniform(third, (L, NTRAIN, 1), jnp.float32) * math.log(10.0))
    return (base * columns * rows_scale / 3.0).astype(jnp.float32)


def level_of(stream_key, dims, cuts, smallest, top_value):
    def one(dim, shards_of):
        heights = jax.random.uniform(jax.random.fold_in(jax.random.fold_in(stream_key, 6), dim), (shards_of,), jnp.float32, smallest / len(cuts), top_value / len(cuts))
        return jnp.repeat(jnp.exp(heights), dims[dim] // shards_of).reshape((-1,) + (1,) * (len(dims) - dim - 1))

    level = one(*cuts[0])
    for cut in cuts[1:]:
        level = level * one(*cut)
    return level


def centred(own_key, shape, spread, limit, pieces=(), held_as=jnp.bfloat16):
    factor_of = level_of(own_key, shape, pieces, -0.22, 0.18) if pieces else 1.0
    array = jax.random.normal(own_key, shape, jnp.float32) * spread * factor_of
    return jnp.minimum(jnp.maximum(array, -limit), limit).astype(held_as)


def setup_inputs(seed: int = 0, part: int = 0) -> dict:
    arg_keys = jax.random.split(jax.random.key(seed), 3)
    own_keys = jax.random.split(jax.random.fold_in(arg_keys[2], part), 3)
    return {
        "train_grads": draw_train_grads(jax.random.fold_in(jax.random.fold_in(arg_keys[2], part), 71), part),
        "query_grads": centred(own_keys[1], (L, NQ, K), 1.0, 6.0, ((1, 16),), jnp.float32),
    }


DAMPING = 0.1


def chebyshev(rhs, hess, lower, upper):
    theta = (upper + lower) / 2.0
    delta = (upper - lower) / 2.0
    sigma = theta / delta

    def step(count, carry):
        solved, resid, direction, rho = carry
        solved = solved + direction
        resid = resid - jnp.dot(direction, hess, precision=lax.Precision.HIGHEST)
        rho_new = 1.0 / (2.0 * sigma - rho)
        direction = rho_new * rho * direction + (2.0 * rho_new / delta) * resid
        return (solved, resid, direction, rho_new)

    start = (jnp.zeros_like(rhs), rhs, rhs / theta, (1.0 / sigma).astype(jnp.float32))
    return lax.fori_loop(0, ITERS, step, start)[0]


def precondition(queries, gram, total_rows):
    width = gram.shape[0]
    damping = DAMPING * jnp.trace(gram) / (total_rows * width)
    hess = gram / total_rows + damping * jnp.eye(width, dtype=jnp.float32)
    upper = jnp.max(jnp.sum(jnp.abs(hess), axis=1))
    return chebyshev(queries, hess, damping, upper)


def reference(train_grads, query_grads):
    total_rows = train_grads.shape[1]
    width = train_grads.shape[2]
    results = []
    for layer in range(L):
        grads = train_grads[layer]
        gram = jnp.einsum("nk,nj->kj", grads, grads, precision=lax.Precision.HIGHEST)
        results.append(precondition(query_grads[layer], gram, total_rows))
    stacked = jnp.stack(results)
    scores = jnp.einsum("lqk,lnk->qn", stacked, train_grads, precision=lax.Precision.HIGHEST)
    return scores * (1.0 / width ** 0.5)
```

```python
import functools

import jax
import jax.numpy as jnp
from jax import lax
from jax.experimental import pallas as pl
from jax.experimental.pallas import tpu as pltpu
from jax.sharding import PartitionSpec as P

ITERS = 12
DAMPING = 0.1
TILE = 128
SPLIT = 4
PIECES = 4

F32 = jnp.float32
BF16 = jnp.bfloat16


def halves(value):
    high = value.astype(BF16)
    return high, (value - high.astype(F32)).astype(BF16)


def dot(left, right, dims):
    return lax.dot_general(left, right, (dims, ((), ())), preferred_element_type=F32)


def remote(src, dst, send, recv, target):
    return pltpu.make_async_remote_copy(
        src_ref=src,
        dst_ref=dst,
        send_sem=send,
        recv_sem=recv,
        device_id={"ex": target},
        device_id_type=pl.DeviceIdType.MESH,
    )


def kernel(
    n, train, query, out,
    rows_f32, high, low, part, acc, sib_buf, y_buf, left_buf, right_buf, full,
    hess, hess_high, hess_low, solved_all, rhs, direction, stacked,
    load_sem, q_send, q_recv, q_local, sib_send, sib_recv, y_send, y_recv, z_send, left_recv, right_recv,
    full_send, full_recv, bz_send, by_send, bs_send, bz_recv, by_recv, bs_recv,
):
    layers, rows, width = train.shape
    depth = query.shape[1]
    strips = width // TILE
    pairs = strips // 2
    mine = pairs // 2
    piece = TILE // SPLIT
    total_rows = rows * n
    half = depth * n // 2
    step_rows = half // PIECES
    chips = n // 4
    root = (chips - 1) // 2

    me = lax.axis_index("ex")
    core = lax.rem(me, 2)
    y = lax.rem(me // 2, 2)
    z = me // 4
    sibling = me + 1 - 2 * core
    across = me + 2 - 4 * y
    is_root = z == root
    my_half = me // (n // 2)
    my_slot = lax.rem(me, n // 2)

    def layer_at(turn):
        return jnp.where(turn == 0, 1 - y, y)

    def load(turn):
        layer = layer_at(turn)
        return pltpu.make_async_copy(train.at[layer], rows_f32.at[turn], load_sem.at[turn])

    load(0).start()
    load(1).start()

    barrier = pltpu.get_barrier_semaphore()

    def greet(j, _):
        pl.semaphore_signal(
            barrier, inc=1, device_id={"ex": lax.rem(me + j, n)}, device_id_type=pl.DeviceIdType.MESH
        )
        return 0

    lax.fori_loop(1, n, greet, 0)
    pl.semaphore_wait(barrier, n - 1)

    def query_copy(layer):
        target = root * 4 + layer * 2 + my_half
        slot = rhs.at[pl.ds(pl.multiple_of(my_slot * depth, 8), depth)]
        return target, query.at[layer], slot

    for layer in range(layers):
        target, src, slot = query_copy(layer)

        @pl.when(target != me)
        def _():
            remote(src, slot, q_send.at[layer], q_recv.at[my_slot], target).start()

        @pl.when(target == me)
        def _():
            pltpu.make_async_copy(src, slot, q_local).start()

    def sib_copy(turn, k):
        return remote(
            part.at[turn, 2 * k + 1 - core], sib_buf.at[turn, k],
            sib_send.at[turn, k], sib_recv.at[turn, k], sibling,
        )

    def y_copy(k, s):
        sl = pl.ds(s * piece, piece)
        return remote(acc.at[0, k, sl], y_buf.at[k, sl], y_send.at[k, s], y_recv.at[k, s], across)

    def left_copy(k, s):
        sl = pl.ds(s * piece, piece)
        return remote(acc.at[1, k, sl], left_buf.at[k, sl], z_send.at[k, s], left_recv.at[k, s], me + 4)

    def right_copy(k, s):
        sl = pl.ds(s * piece, piece)
        return remote(acc.at[1, k, sl], right_buf.at[k, sl], z_send.at[k, s], right_recv.at[k, s], me - 4)

    def full_copy(k, s):
        src = full.at[2 * k + core, pl.ds(s * piece, piece)]
        return remote(src, src, full_send.at[k, s], full_recv.at[k, s], sibling)

    def full_wait(k, s):
        src = full.at[2 * k + 1 - core, pl.ds(s * piece, piece)]
        remote(src, src, full_send.at[k, s], full_recv.at[k, s], sibling).wait_recv()

    def merge(turn, k):
        sib_copy(turn, k).wait_recv()
        acc[turn, k] = part[turn, 2 * k + core] + sib_buf[turn, k]

        @pl.when(turn == 0)
        def _():
            for s in range(SPLIT):
                y_copy(k, s).start()

    def gram(turn, _):
        load(turn).wait()

        def cut(b, _):
            sl = pl.ds(pl.multiple_of(b * TILE, TILE), TILE)
            high[turn, sl], low[turn, sl] = halves(rows_f32[turn, sl])
            return 0

        lax.fori_loop(0, rows // TILE, cut, 0)
        for p in range(pairs):
            column = 0
            for i in (p, strips - 1 - p):
                span = (strips - i) * TILE
                lo, hi = i * TILE, (i + 1) * TILE
                left_high = high[turn, :, lo:hi]
                left_low = low[turn, :, lo:hi]
                right_high = high[turn, :, lo:]
                right_low = low[turn, :, lo:]
                dims = ((0,), (0,))
                part[turn, p, :, column:column + span] = (
                    dot(left_high, right_low, dims) + dot(left_low, right_high, dims)
                ) + dot(left_high, right_high, dims)
                column += span

            @pl.when(core != p % 2)
            def _():
                sib_copy(turn, p // 2).start()

            if p >= 2 and p % 2 == 0:
                merge(turn, p // 2 - 1)
        merge(turn, mine - 1)
        return 0

    lax.fori_loop(0, 2, gram, 0)

    from_left = jnp.logical_and(z > 0, z <= root)
    from_right = jnp.logical_and(z < chips - 1, z >= root)
    for k in range(mine):
        for s in range(SPLIT):
            sl = pl.ds(s * piece, piece)
            y_copy(k, s).wait_recv()
            acc[1, k, sl] = acc[1, k, sl] + y_buf[k, sl]

            @pl.when(from_left)
            def _():
                left_copy(k, s).wait_recv()
                acc[1, k, sl] = acc[1, k, sl] + left_buf[k, sl]

            @pl.when(from_right)
            def _():
                right_copy(k, s).wait_recv()
                acc[1, k, sl] = acc[1, k, sl] + right_buf[k, sl]

            @pl.when(z < root)
            def _():
                left_copy(k, s).start()

            @pl.when(z > root)
            def _():
                right_copy(k, s).start()

            @pl.when(is_root)
            def _():
                full[2 * k + core, sl] = acc[1, k, sl]
                full_copy(k, s).start()

    def part_of(layer, h, b):
        return solved_all.at[layer, pl.ds(pl.multiple_of(h * half + b * step_rows, 8), step_rows)]

    def down_copy(b, sem, target):
        ref = part_of(y, core, b)
        return remote(ref, ref, bz_send.at[sem, b], bz_recv.at[b], target)

    def over_copy(b):
        ref = part_of(y, core, b)
        return remote(ref, ref, by_send.at[b], by_recv.at[b], across)

    def over_wait(b):
        ref = part_of(1 - y, core, b)
        remote(ref, ref, by_send.at[b], by_recv.at[b], across).wait_recv()

    def share_copy(turn, b):
        ref = part_of(layer_at(turn), core, b)
        return remote(ref, ref, bs_send.at[turn, b], bs_recv.at[turn, b], sibling)

    def share_wait(turn, b):
        ref = part_of(layer_at(turn), 1 - core, b)
        remote(ref, ref, bs_send.at[turn, b], bs_recv.at[turn, b], sibling).wait_recv()

    @pl.when(is_root)
    def _():
        for k in range(mine):
            for s in range(SPLIT):
                full_wait(k, s)
        eye = (
            lax.broadcasted_iota(jnp.int32, (TILE, TILE), 0)
            == lax.broadcasted_iota(jnp.int32, (TILE, TILE), 1)
        ).astype(F32)
        diagonal = jnp.zeros((TILE, TILE), F32)
        for i in range(strips):
            p = min(i, strips - 1 - i)
            start = 0 if i == p else (strips - p) * TILE
            lo, hi = i * TILE, (i + 1) * TILE
            strip = full[p, :, start:start + (strips - i) * TILE]
            diagonal = diagonal + strip[:, :TILE] * eye
            strip = strip * (1.0 / total_rows)
            hess[lo:hi, lo:] = strip
            if i < strips - 1:
                hess[hi:, lo:hi] = strip[:, TILE:].T
        trace = jnp.sum(jnp.sum(diagonal, axis=0, keepdims=True), axis=1, keepdims=True)
        damping = trace * (DAMPING / (total_rows * width))
        sums = jnp.zeros((1, width), F32)
        for i in range(strips):
            lo, hi = i * TILE, (i + 1) * TILE
            hess[lo:hi, lo:hi] = hess[lo:hi, lo:hi] + damping * eye
            block = hess[lo:hi, :]
            sums = sums + jnp.sum(jnp.abs(block), axis=0, keepdims=True)
            hess_high[lo:hi, :], hess_low[lo:hi, :] = halves(block)
        upper = jnp.max(sums, axis=1, keepdims=True)
        theta = (upper + damping) / 2.0
        delta = (upper - damping) / 2.0
        sigma = theta / delta

        for j in range(n // 2):
            at = pl.ds(j * depth, depth)
            source = (y * 0 + core) * (n // 2) + j
            waiting = remote(query.at[0], rhs.at[at], q_send.at[0], q_recv.at[j], sibling)

            @pl.when(source != me)
            def _():
                waiting.wait_recv()

            @pl.when(source == me)
            def _():
                pltpu.make_async_copy(query.at[0], rhs.at[at], q_local).wait()

        mine_rows = pl.ds(pl.multiple_of(core * half, 8), half)
        solved_all[y, mine_rows] = jnp.zeros((half, width), F32)
        direction[...] = rhs[...] / theta

        def step(_, rho):
            current = direction[...]
            solved_all[y, mine_rows] = solved_all[y, mine_rows] + current
            stacked[0:half], stacked[half:2 * half] = halves(current)
            dims = ((1,), (0,))
            wide = dot(stacked[0:2 * half], hess_high[...], dims)
            product = wide[:half] + (wide[half:] + dot(stacked[0:half], hess_low[...], dims))
            resid = rhs[...] - product
            rhs[...] = resid
            rho_new = 1.0 / (2.0 * sigma - rho)
            direction[...] = rho_new * rho * current + (2.0 * rho_new / delta) * resid
            return rho_new

        lax.fori_loop(0, ITERS - 1, step, 1.0 / sigma)
        solved_all[y, mine_rows] = solved_all[y, mine_rows] + direction[...]

    for b in range(PIECES):
        @pl.when(jnp.logical_not(is_root))
        def _():
            down_copy(b, 0, me).wait_recv()

        @pl.when(jnp.logical_and(z <= root, z > 0))
        def _():
            down_copy(b, 0, me - 4).start()

        @pl.when(jnp.logical_and(z >= root, z < chips - 1))
        def _():
            down_copy(b, 1, me + 4).start()

        over_copy(b).start()
        share_copy(1, b).start()
    for b in range(PIECES):
        over_wait(b)
        share_copy(0, b).start()
    for b in range(PIECES):
        share_wait(1, b)
        share_wait(0, b)

    scale = 1.0 / width ** 0.5
    block_rows = min(rows, 2 * TILE)
    count = 2 * half
    for turn in range(2):
        layer = layer_at(turn)
        stacked[0:count], stacked[count:2 * count] = halves(solved_all[layer])

        def score(b, _):
            at = pl.ds(pl.multiple_of(b * block_rows, block_rows), block_rows)
            dims = ((1,), (1,))
            wide = dot(stacked[...], high[turn, at], dims)
            value = wide[:count] + (wide[count:] + dot(stacked[0:count], low[turn, at], dims))
            if turn == 0:
                out[:, at] = value
            else:
                out[:, at] = (out[:, at] + value) * scale
            return 0

        lax.fori_loop(0, rows // block_rows, score, 0)

    for layer in range(layers):
        target, src, slot = query_copy(layer)

        @pl.when(target != me)
        def _():
            remote(src, slot, q_send.at[layer], q_recv.at[my_slot], target).wait_send()

    for k in range(mine):
        for turn in range(2):
            sib_copy(turn, k).wait_send()
        for s in range(SPLIT):
            y_copy(k, s).wait_send()

            @pl.when(z < root)
            def _():
                left_copy(k, s).wait_send()

            @pl.when(z > root)
            def _():
                right_copy(k, s).wait_send()

            @pl.when(is_root)
            def _():
                full_copy(k, s).wait_send()

    for b in range(PIECES):
        @pl.when(jnp.logical_and(z <= root, z > 0))
        def _():
            down_copy(b, 0, me - 4).wait_send()

        @pl.when(jnp.logical_and(z >= root, z < chips - 1))
        def _():
            down_copy(b, 1, me + 4).wait_send()

        over_copy(b).wait_send()
        share_copy(1, b).wait_send()
        share_copy(0, b).wait_send()


def shards(n, train_grads, query_grads):
    layers, rows, width = train_grads.shape
    depth = query_grads.shape[1]
    strips = width // TILE
    pairs, span = strips // 2, (strips + 1) * TILE
    mine = pairs // 2
    count = n * depth
    half = count // 2
    dma = pltpu.SemaphoreType.DMA
    return pl.pallas_call(
        functools.partial(kernel, n),
        out_shape=jax.ShapeDtypeStruct((count, rows), F32),
        in_specs=[
            pl.BlockSpec(memory_space=pl.ANY),
            pl.BlockSpec(memory_space=pltpu.VMEM),
        ],
        out_specs=pl.BlockSpec(memory_space=pltpu.VMEM),
        scratch_shapes=[
            pltpu.VMEM((layers, rows, width), F32),
            pltpu.VMEM((layers, rows, width), BF16),
            pltpu.VMEM((layers, rows, width), BF16),
            pltpu.VMEM((layers, pairs, TILE, span), F32),
            pltpu.VMEM((layers, mine, TILE, span), F32),
            pltpu.VMEM((layers, mine, TILE, span), F32),
            pltpu.VMEM((mine, TILE, span), F32),
            pltpu.VMEM((mine, TILE, span), F32),
            pltpu.VMEM((mine, TILE, span), F32),
            pltpu.VMEM((pairs, TILE, span), F32),
            pltpu.VMEM((width, width), F32),
            pltpu.VMEM((width, width), BF16),
            pltpu.VMEM((width, width), BF16),
            pltpu.VMEM((layers, count, width), F32),
            pltpu.VMEM((half, width), F32),
            pltpu.VMEM((half, width), F32),
            pltpu.VMEM((2 * count, width), BF16),
            dma((2,)), dma((layers,)), dma((n // 2,)), dma,
            dma((2, mine)), dma((2, mine)),
            dma((mine, SPLIT)), dma((mine, SPLIT)),
            dma((mine, SPLIT)), dma((mine, SPLIT)), dma((mine, SPLIT)),
            dma((mine, SPLIT)), dma((mine, SPLIT)),
            dma((2, PIECES)), dma((PIECES,)), dma((2, PIECES)),
            dma((PIECES,)), dma((PIECES,)), dma((2, PIECES)),
        ],
        compiler_params=pltpu.CompilerParams(
            collective_id=0, has_side_effects=True, vmem_limit_bytes=60 * 1024 * 1024
        ),
    )(train_grads, query_grads)


def solution(mesh):
    in_specs = (P(None, ("parts", "ex"), None), P(None, ("parts", "ex"), None))
    out_specs = P(None, ("parts", "ex"))
    return jax.shard_map(
        functools.partial(shards, mesh.shape["ex"]),
        mesh=mesh, in_specs=in_specs, out_specs=out_specs, check_vma=False,
    )
```

```python
import functools

import jax
import jax.numpy as jnp
from jax import lax
from jax.experimental import pallas as pl
from jax.experimental.pallas import tpu as pltpu
from jax.sharding import PartitionSpec as P

ITERS = 12
DAMPING = 0.1
TILE = 128
SPLIT = 2
PIECES = 4
B_WINDOW = 4
WINDOW = 4

F32 = jnp.float32
BF16 = jnp.bfloat16


def halves(value):
    high = value.astype(BF16)
    return high, (value - high.astype(F32)).astype(BF16)


def dot(left, right, dims):
    return lax.dot_general(left, right, (dims, ((), ())), preferred_element_type=F32)


def remote(src, dst, send, recv, target):
    return pltpu.make_async_remote_copy(
        src_ref=src,
        dst_ref=dst,
        send_sem=send,
        recv_sem=recv,
        device_id={"ex": target},
        device_id_type=pl.DeviceIdType.MESH,
    )


def kernel(
    n, train, query, out,
    rows_f32, high, low, part, acc, sib_buf, y_buf, left_buf, right_buf, full,
    corner, sums, hess_high, hess_low, solved_all, rhs, direction, stacked,
    load_sem, q_send, q_recv, q_local, sib_send, sib_recv, y_send, y_recv, z_send, left_recv, right_recv,
    full_send, full_recv, bz_send, by_send, bs_send, bz_recv, by_recv, bs_recv,
):
    layers, rows, width = train.shape
    depth = query.shape[1]
    strips = width // TILE
    pairs = strips // 2
    share = TILE // 2
    piece = share // SPLIT
    total_rows = rows * n
    half = depth * n // 2
    step_rows = half // PIECES
    chips = n // 4
    root = (chips - 1) // 2

    me = lax.axis_index("ex")
    core = lax.rem(me, 2)
    y = lax.rem(me // 2, 2)
    z = me // 4
    sibling = me + 1 - 2 * core
    across = me + 2 - 4 * y
    is_root = z == root
    my_half = me // (n // 2)
    my_slot = lax.rem(me, n // 2)

    def layer_at(turn):
        return jnp.where(turn == 0, 1 - y, y)

    def load(turn):
        layer = layer_at(turn)
        return pltpu.make_async_copy(train.at[layer], rows_f32.at[turn], load_sem.at[turn])

    load(0).start()
    load(1).start()

    barrier = pltpu.get_barrier_semaphore()

    def greet(j, _):
        pl.semaphore_signal(
            barrier, inc=1, device_id={"ex": lax.rem(me + j, n)}, device_id_type=pl.DeviceIdType.MESH
        )
        return 0

    lax.fori_loop(1, n, greet, 0)

    def query_copy(layer):
        target = root * 4 + layer * 2 + my_half
        slot = rhs.at[pl.ds(pl.multiple_of(my_slot * depth, 8), depth)]
        return target, query.at[layer], slot

    def send_queries():
        for layer in range(layers):
            target, src, slot = query_copy(layer)

            @pl.when(target != me)
            def _():
                remote(src, slot, q_send.at[layer], q_recv.at[my_slot], target).start()

            @pl.when(target == me)
            def _():
                pltpu.make_async_copy(src, slot, q_local).start()

    def sib_copy(turn, k):
        return remote(
            part.at[turn, k, pl.ds(pl.multiple_of((1 - core) * share, 8), share)], sib_buf.at[turn, k],
            sib_send.at[turn, k], sib_recv.at[turn, k], sibling,
        )

    def y_copy(k, s):
        sl = pl.ds(s * piece, piece)
        return remote(acc.at[0, k, sl], y_buf.at[k, sl], y_send.at[k, s], y_recv.at[k, s], across)

    def left_copy(k, s):
        sl = pl.ds(s * piece, piece)
        return remote(acc.at[1, k, sl], left_buf.at[k, sl], z_send.at[k, s], left_recv.at[k, s], me + 4)

    def right_copy(k, s):
        sl = pl.ds(s * piece, piece)
        return remote(acc.at[1, k, sl], right_buf.at[k, sl], z_send.at[k, s], right_recv.at[k, s], me - 4)

    def full_copy(k, s):
        src = full.at[k, pl.ds(pl.multiple_of(core * share + s * piece, 8), piece)]
        return remote(src, src, full_send.at[k, s], full_recv.at[k, s], sibling)

    def full_wait(k, s):
        src = full.at[k, pl.ds(pl.multiple_of((1 - core) * share + s * piece, 8), piece)]
        remote(src, src, full_send.at[k, s], full_recv.at[k, s], sibling).wait_recv()

    def merge(turn, k):
        sib_copy(turn, k).wait_recv()
        acc[turn, k] = part[turn, k, pl.ds(pl.multiple_of(core * share, 8), share)] + sib_buf[turn, k]

        @pl.when(turn == 0)
        def _():
            for s in range(SPLIT):
                if k * SPLIT + s < WINDOW:
                    y_copy(k, s).start()

    def pump(m):
        if m < pairs * SPLIT - WINDOW:
            y_copy(m // SPLIT, m % SPLIT).wait_send()
            y_copy((m + WINDOW) // SPLIT, (m + WINDOW) % SPLIT).start()

    eye = (
        lax.broadcasted_iota(jnp.int32, (TILE, TILE), 0)
        == lax.broadcasted_iota(jnp.int32, (TILE, TILE), 1)
    ).astype(F32)

    def assemble(k):
        if k == 0:
            sums[...] = jnp.zeros_like(sums)
        column = 0
        for i in (k, strips - 1 - k):
            span = (strips - i) * TILE
            lo, hi = i * TILE, (i + 1) * TILE
            corner[i] = full[k, :, column:column + TILE] * (1.0 / total_rows)
            if i < strips - 1:
                strip = full[k, :, column + TILE:column + span] * (1.0 / total_rows)
                turned = strip.T
                hess_high[lo:hi, hi:], hess_low[lo:hi, hi:] = halves(strip)
                hess_high[hi:, lo:hi], hess_low[hi:, lo:hi] = halves(turned)
                sums[0:1, hi:] += jnp.sum(jnp.abs(strip), axis=0, keepdims=True)
                sums[0:1, lo:hi] += jnp.sum(jnp.abs(turned), axis=0, keepdims=True)
            column += span

    from_left = jnp.logical_and(z > 0, z <= root)
    from_right = jnp.logical_and(z < chips - 1, z >= root)
    def chain(k):
        for s in range(SPLIT):
            sl = pl.ds(s * piece, piece)
            y_copy(k, s).wait_recv()
            pump(k * SPLIT + s)
            acc[1, k, sl] = acc[1, k, sl] + y_buf[k, sl]

            @pl.when(from_left)
            def _():
                left_copy(k, s).wait_recv()
                acc[1, k, sl] = acc[1, k, sl] + left_buf[k, sl]

            @pl.when(from_right)
            def _():
                right_copy(k, s).wait_recv()
                acc[1, k, sl] = acc[1, k, sl] + right_buf[k, sl]

            @pl.when(z < root)
            def _():
                left_copy(k, s).start()

            @pl.when(z > root)
            def _():
                right_copy(k, s).start()

            @pl.when(is_root)
            def _():
                full[k, pl.ds(pl.multiple_of(core * share + s * piece, 8), piece)] = acc[1, k, sl]
                full_copy(k, s).start()

    def gather(k):
        @pl.when(is_root)
        def _():
            for s in range(SPLIT):
                full_wait(k, s)
            assemble(k)

    def prepare(turn):
        load(turn).wait()

        def cut(b, _):
            sl = pl.ds(pl.multiple_of(b * TILE, TILE), TILE)
            high[turn, sl], low[turn, sl] = halves(rows_f32[turn, sl])
            return 0

        lax.fori_loop(0, rows // TILE, cut, 0)

    def multiply(turn, p):
        column = 0
        for i in (p, strips - 1 - p):
            span = (strips - i) * TILE
            lo, hi = i * TILE, (i + 1) * TILE
            left_high = high[turn, :, lo:hi]
            left_low = low[turn, :, lo:hi]
            right_high = high[turn, :, lo:]
            right_low = low[turn, :, lo:]
            dims = ((0,), (0,))
            part[turn, p, :, column:column + span] = (
                dot(left_high, right_low, dims) + dot(left_low, right_high, dims)
            ) + dot(left_high, right_high, dims)
            column += span

    def gram(turn, _):
        for p in range(pairs):
            if p == 0:
                @pl.when(turn == 1)
                def _():
                    prepare(1)
                    multiply(1, 0)
            else:
                multiply(turn, p)
            sib_copy(turn, p).start()
            if p >= 1:
                merge(turn, p - 1)
            if p >= 2:
                @pl.when(turn == 1)
                def _():
                    chain(p - 2)
        merge(turn, pairs - 1)
        return 0

    prepare(0)
    multiply(0, 0)
    pl.semaphore_wait(barrier, n - 1)
    send_queries()
    lax.fori_loop(0, 2, gram, 0)

    gather(0)
    for k in range(pairs - 2, pairs):
        chain(k)
        gather(k - 1)
    gather(pairs - 1)

    def part_of(layer, h, b):
        return solved_all.at[layer, pl.ds(pl.multiple_of(h * half + b * step_rows, 8), step_rows)]

    def down_copy(b, sem, target):
        ref = part_of(y, core, b)
        return remote(ref, ref, bz_send.at[sem, b], bz_recv.at[b], target)

    def over_copy(b):
        ref = part_of(y, core, b)
        return remote(ref, ref, by_send.at[b], by_recv.at[b], across)

    def over_wait(b):
        ref = part_of(1 - y, core, b)
        remote(ref, ref, by_send.at[b], by_recv.at[b], across).wait_recv()

    def share_copy(turn, b):
        ref = part_of(layer_at(turn), core, b)
        return remote(ref, ref, bs_send.at[turn, b], bs_recv.at[turn, b], sibling)

    def share_wait(turn, b):
        ref = part_of(layer_at(turn), 1 - core, b)
        remote(ref, ref, bs_send.at[turn, b], bs_recv.at[turn, b], sibling).wait_recv()

    @pl.when(is_root)
    def _():
        diagonal = jnp.zeros((TILE, TILE), F32)
        for i in range(strips):
            diagonal = diagonal + corner[i] * eye
        trace = jnp.sum(jnp.sum(diagonal, axis=0, keepdims=True), axis=1, keepdims=True)
        damping = trace * (DAMPING / width)
        for i in range(strips):
            lo, hi = i * TILE, (i + 1) * TILE
            block = corner[i] + damping * eye
            sums[0:1, lo:hi] += jnp.sum(jnp.abs(block), axis=0, keepdims=True)
            hess_high[lo:hi, lo:hi], hess_low[lo:hi, lo:hi] = halves(block)
        upper = jnp.max(sums[0:1], axis=1, keepdims=True)
        theta = (upper + damping) / 2.0
        delta = (upper - damping) / 2.0
        sigma = theta / delta

        for j in range(n // 2):
            at = pl.ds(j * depth, depth)
            source = (y * 0 + core) * (n // 2) + j
            waiting = remote(query.at[0], rhs.at[at], q_send.at[0], q_recv.at[j], sibling)

            @pl.when(source != me)
            def _():
                waiting.wait_recv()

            @pl.when(source == me)
            def _():
                pltpu.make_async_copy(query.at[0], rhs.at[at], q_local).wait()

        mine_rows = pl.ds(pl.multiple_of(core * half, 8), half)
        solved_all[y, mine_rows] = jnp.zeros((half, width), F32)
        direction[...] = rhs[...] / theta

        def step(_, rho):
            current = direction[...]
            solved_all[y, mine_rows] = solved_all[y, mine_rows] + current
            stacked[0:half], stacked[half:2 * half] = halves(current)
            dims = ((1,), (0,))
            wide = dot(stacked[0:2 * half], hess_high[...], dims)
            product = wide[:half] + (wide[half:] + dot(stacked[0:half], hess_low[...], dims))
            resid = rhs[...] - product
            rhs[...] = resid
            rho_new = 1.0 / (2.0 * sigma - rho)
            direction[...] = rho_new * rho * current + (2.0 * rho_new / delta) * resid
            return rho_new

        lax.fori_loop(0, ITERS - 1, step, 1.0 / sigma)
        solved_all[y, mine_rows] = solved_all[y, mine_rows] + direction[...]

    def sent(b):
        @pl.when(jnp.logical_and(z <= root, z > 0))
        def _():
            down_copy(b, 0, me - 4).wait_send()

        @pl.when(jnp.logical_and(z >= root, z < chips - 1))
        def _():
            down_copy(b, 1, me + 4).wait_send()

        over_copy(b).wait_send()
        share_copy(1, b).wait_send()

    for b in range(PIECES):
        @pl.when(jnp.logical_not(is_root))
        def _():
            down_copy(b, 0, me).wait_recv()

        if b >= B_WINDOW:
            sent(b - B_WINDOW)

        @pl.when(jnp.logical_and(z <= root, z > 0))
        def _():
            down_copy(b, 0, me - 4).start()

        @pl.when(jnp.logical_and(z >= root, z < chips - 1))
        def _():
            down_copy(b, 1, me + 4).start()

        over_copy(b).start()
        share_copy(1, b).start()
        if b >= 1:
            over_wait(b - 1)
            share_copy(0, b - 1).start()
    over_wait(PIECES - 1)
    share_copy(0, PIECES - 1).start()
    for b in range(PIECES):
        share_wait(1, b)
        share_wait(0, b)

    scale = 1.0 / width ** 0.5
    block_rows = min(rows, 2 * TILE)
    count = 2 * half
    for turn in range(2):
        layer = layer_at(turn)
        stacked[0:count], stacked[count:2 * count] = halves(solved_all[layer])

        def score(b, _):
            at = pl.ds(pl.multiple_of(b * block_rows, block_rows), block_rows)
            dims = ((1,), (1,))
            wide = dot(stacked[...], high[turn, at], dims)
            value = wide[:count] + (wide[count:] + dot(stacked[0:count], low[turn, at], dims))
            if turn == 0:
                out[:, at] = value
            else:
                out[:, at] = (out[:, at] + value) * scale
            return 0

        lax.fori_loop(0, rows // block_rows, score, 0)

    for layer in range(layers):
        target, src, slot = query_copy(layer)

        @pl.when(target != me)
        def _():
            remote(src, slot, q_send.at[layer], q_recv.at[my_slot], target).wait_send()

    for k in range(pairs):
        for turn in range(2):
            sib_copy(turn, k).wait_send()
        for s in range(SPLIT):
            if k * SPLIT + s >= pairs * SPLIT - WINDOW:
                y_copy(k, s).wait_send()

            @pl.when(z < root)
            def _():
                left_copy(k, s).wait_send()

            @pl.when(z > root)
            def _():
                right_copy(k, s).wait_send()

            @pl.when(is_root)
            def _():
                full_copy(k, s).wait_send()

    for b in range(PIECES - B_WINDOW, PIECES):
        sent(b)
    for b in range(PIECES):
        share_copy(0, b).wait_send()


def shards(n, train_grads, query_grads):
    layers, rows, width = train_grads.shape
    depth = query_grads.shape[1]
    strips = width // TILE
    pairs, span = strips // 2, (strips + 1) * TILE
    share = TILE // 2
    count = n * depth
    half = count // 2
    dma = pltpu.SemaphoreType.DMA
    return pl.pallas_call(
        functools.partial(kernel, n),
        out_shape=jax.ShapeDtypeStruct((count, rows), F32),
        in_specs=[
            pl.BlockSpec(memory_space=pl.ANY),
            pl.BlockSpec(memory_space=pltpu.VMEM),
        ],
        out_specs=pl.BlockSpec(memory_space=pltpu.VMEM),
        scratch_shapes=[
            pltpu.VMEM((layers, rows, width), F32),
            pltpu.VMEM((layers, rows, width), BF16),
            pltpu.VMEM((layers, rows, width), BF16),
            pltpu.VMEM((layers, pairs, TILE, span), F32),
            pltpu.VMEM((layers, pairs, share, span), F32),
            pltpu.VMEM((layers, pairs, share, span), F32),
            pltpu.VMEM((pairs, share, span), F32),
            pltpu.VMEM((pairs, share, span), F32),
            pltpu.VMEM((pairs, share, span), F32),
            pltpu.VMEM((pairs, TILE, span), F32),
            pltpu.VMEM((strips, TILE, TILE), F32),
            pltpu.VMEM((8, width), F32),
            pltpu.VMEM((width, width), BF16),
            pltpu.VMEM((width, width), BF16),
            pltpu.VMEM((layers, count, width), F32),
            pltpu.VMEM((half, width), F32),
            pltpu.VMEM((half, width), F32),
            pltpu.VMEM((2 * count, width), BF16),
            dma((2,)), dma((layers,)), dma((n // 2,)), dma,
            dma((2, pairs)), dma((2, pairs)),
            dma((pairs, SPLIT)), dma((pairs, SPLIT)),
            dma((pairs, SPLIT)), dma((pairs, SPLIT)), dma((pairs, SPLIT)),
            dma((pairs, SPLIT)), dma((pairs, SPLIT)),
            dma((2, PIECES)), dma((PIECES,)), dma((2, PIECES)),
            dma((PIECES,)), dma((PIECES,)), dma((2, PIECES)),
        ],
        compiler_params=pltpu.CompilerParams(
            collective_id=0, has_side_effects=True, vmem_limit_bytes=60 * 1024 * 1024
        ),
    )(train_grads, query_grads)


def solution(mesh):
    in_specs = (P(None, ("parts", "ex"), None), P(None, ("parts", "ex"), None))
    out_specs = P(None, ("parts", "ex"))
    return jax.shard_map(
        functools.partial(shards, mesh.shape["ex"]),
        mesh=mesh, in_specs=in_specs, out_specs=out_specs, check_vma=False,
    )
```

```python
import functools

import jax
import jax.numpy as jnp
from jax import lax
from jax.experimental import pallas as pl
from jax.experimental.pallas import tpu as pltpu
from jax.sharding import PartitionSpec as P

ITERS = 12
DAMPING = 0.1
TILE = 128
SPLIT = 2
PIECES = 4
B_WINDOW = 4
WINDOW = 4

F32 = jnp.float32
BF16 = jnp.bfloat16


def halves(value):
    high = value.astype(BF16)
    return high, (value - high.astype(F32)).astype(BF16)


def dot(left, right, dims):
    return lax.dot_general(left, right, (dims, ((), ())), preferred_element_type=F32)


def remote(src, dst, send, recv, target):
    return pltpu.make_async_remote_copy(
        src_ref=src,
        dst_ref=dst,
        send_sem=send,
        recv_sem=recv,
        device_id={"ex": target},
        device_id_type=pl.DeviceIdType.MESH,
    )


def kernel(
    n, train, query, out,
    rows_f32, high, low, part, acc, sib_buf, y_buf, left_buf, right_buf, full,
    corner, sums, hess_high, hess_low, solved_all, rhs, direction, stacked,
    load_sem, q_send, q_recv, q_local, sib_send, sib_recv, y_send, y_recv, z_send, left_recv, right_recv,
    full_send, full_recv, bz_send, by_send, bs_send, bz_recv, by_recv, bs_recv,
):
    layers, rows, width = train.shape
    depth = query.shape[1]
    strips = width // TILE
    pairs = strips // 2
    share = TILE // 2
    piece = share // SPLIT
    total_rows = rows * n
    half = depth * n // 2
    step_rows = half // PIECES
    chips = n // 4
    root = (chips - 1) // 2

    me = lax.axis_index("ex")
    core = lax.rem(me, 2)
    y = lax.rem(me // 2, 2)
    z = me // 4
    sibling = me + 1 - 2 * core
    across = me + 2 - 4 * y
    is_root = z == root
    my_half = me // (n // 2)
    my_slot = lax.rem(me, n // 2)

    def layer_at(turn):
        return jnp.where(turn == 0, 1 - y, y)

    def load(turn):
        layer = layer_at(turn)
        return pltpu.make_async_copy(train.at[layer], rows_f32.at[turn], load_sem.at[turn])

    load(0).start()
    load(1).start()

    barrier = pltpu.get_barrier_semaphore()

    def greet(j, _):
        pl.semaphore_signal(
            barrier, inc=1, device_id={"ex": lax.rem(me + j, n)}, device_id_type=pl.DeviceIdType.MESH
        )
        return 0

    lax.fori_loop(1, n, greet, 0)

    def query_copy(layer):
        target = root * 4 + layer * 2 + my_half
        slot = rhs.at[pl.ds(pl.multiple_of(my_slot * depth, 8), depth)]
        return target, query.at[layer], slot

    def send_queries():
        for layer in range(layers):
            target, src, slot = query_copy(layer)

            @pl.when(target != me)
            def _():
                remote(src, slot, q_send.at[layer], q_recv.at[my_slot], target).start()

            @pl.when(target == me)
            def _():
                pltpu.make_async_copy(src, slot, q_local).start()

    def sib_copy(turn, k):
        return remote(
            part.at[turn, k, pl.ds(pl.multiple_of((1 - core) * share, 8), share)], sib_buf.at[turn, k],
            sib_send.at[turn, k], sib_recv.at[turn, k], sibling,
        )

    def y_copy(k, s):
        sl = pl.ds(s * piece, piece)
        return remote(acc.at[0, k, sl], y_buf.at[k, sl], y_send.at[k, s], y_recv.at[k, s], across)

    def left_copy(k, s):
        sl = pl.ds(s * piece, piece)
        return remote(acc.at[1, k, sl], left_buf.at[k, sl], z_send.at[k, s], left_recv.at[k, s], me + 4)

    def right_copy(k, s):
        sl = pl.ds(s * piece, piece)
        return remote(acc.at[1, k, sl], right_buf.at[k, sl], z_send.at[k, s], right_recv.at[k, s], me - 4)

    def full_copy(k, s):
        src = full.at[k, pl.ds(pl.multiple_of(core * share + s * piece, 8), piece)]
        return remote(src, src, full_send.at[k, s], full_recv.at[k, s], sibling)

    def full_wait(k, s):
        src = full.at[k, pl.ds(pl.multiple_of((1 - core) * share + s * piece, 8), piece)]
        remote(src, src, full_send.at[k, s], full_recv.at[k, s], sibling).wait_recv()

    def merge(turn, k):
        sib_copy(turn, k).wait_recv()
        acc[turn, k] = part[turn, k, pl.ds(pl.multiple_of(core * share, 8), share)] + sib_buf[turn, k]

        @pl.when(turn == 0)
        def _():
            for s in range(SPLIT):
                if k * SPLIT + s < WINDOW:
                    y_copy(k, s).start()

    def pump(m):
        if m < pairs * SPLIT - WINDOW:
            y_copy(m // SPLIT, m % SPLIT).wait_send()
            y_copy((m + WINDOW) // SPLIT, (m + WINDOW) % SPLIT).start()

    eye = (
        lax.broadcasted_iota(jnp.int32, (TILE, TILE), 0)
        == lax.broadcasted_iota(jnp.int32, (TILE, TILE), 1)
    ).astype(F32)

    def assemble(k):
        if k == 0:
            sums[...] = jnp.zeros_like(sums)
        column = 0
        for i in (k, strips - 1 - k):
            span = (strips - i) * TILE
            lo, hi = i * TILE, (i + 1) * TILE
            corner[i] = full[k, :, column:column + TILE] * (1.0 / total_rows)
            if i < strips - 1:
                strip = full[k, :, column + TILE:column + span] * (1.0 / total_rows)
                turned = strip.T
                hess_high[lo:hi, hi:], hess_low[lo:hi, hi:] = halves(strip)
                hess_high[hi:, lo:hi], hess_low[hi:, lo:hi] = halves(turned)
                sums[0:1, hi:] += jnp.sum(jnp.abs(strip), axis=0, keepdims=True)
                sums[0:1, lo:hi] += jnp.sum(jnp.abs(turned), axis=0, keepdims=True)
            column += span

    from_left = jnp.logical_and(z > 0, z <= root)
    from_right = jnp.logical_and(z < chips - 1, z >= root)
    def chain(k):
        for s in range(SPLIT):
            sl = pl.ds(s * piece, piece)
            y_copy(k, s).wait_recv()
            pump(k * SPLIT + s)
            acc[1, k, sl] = acc[1, k, sl] + y_buf[k, sl]

            @pl.when(from_left)
            def _():
                left_copy(k, s).wait_recv()
                acc[1, k, sl] = acc[1, k, sl] + left_buf[k, sl]

            @pl.when(from_right)
            def _():
                right_copy(k, s).wait_recv()
                acc[1, k, sl] = acc[1, k, sl] + right_buf[k, sl]

            @pl.when(z < root)
            def _():
                left_copy(k, s).start()

            @pl.when(z > root)
            def _():
                right_copy(k, s).start()

            @pl.when(is_root)
            def _():
                full[k, pl.ds(pl.multiple_of(core * share + s * piece, 8), piece)] = acc[1, k, sl]
                full_copy(k, s).start()

    def gather(k):
        @pl.when(is_root)
        def _():
            for s in range(SPLIT):
                full_wait(k, s)
            assemble(k)

    def prepare(turn):
        load(turn).wait()

        def cut(b, _):
            sl = pl.ds(pl.multiple_of(b * TILE, TILE), TILE)
            high[turn, sl], low[turn, sl] = halves(rows_f32[turn, sl])
            return 0

        lax.fori_loop(0, rows // TILE, cut, 0)

    def multiply(turn, p):
        column = 0
        for i in (p, strips - 1 - p):
            span = (strips - i) * TILE
            lo, hi = i * TILE, (i + 1) * TILE
            left_high = high[turn, :, lo:hi]
            left_low = low[turn, :, lo:hi]
            right_high = high[turn, :, lo:]
            right_low = low[turn, :, lo:]
            dims = ((0,), (0,))
            part[turn, p, :, column:column + span] = (
                dot(left_high, right_low, dims) + dot(left_low, right_high, dims)
            ) + dot(left_high, right_high, dims)
            column += span

    def gram(turn, _):
        for p in range(pairs):
            if p == 0:
                @pl.when(turn == 1)
                def _():
                    prepare(1)
                    multiply(1, 0)
            else:
                multiply(turn, p)
            sib_copy(turn, p).start()
            if p >= 1:
                merge(turn, p - 1)
            if p >= 2:
                @pl.when(turn == 1)
                def _():
                    chain(p - 2)
        merge(turn, pairs - 1)
        return 0

    prepare(0)
    multiply(0, 0)
    pl.semaphore_wait(barrier, n - 1)
    send_queries()
    lax.fori_loop(0, 2, gram, 0)

    gather(0)
    for k in range(pairs - 2, pairs):
        chain(k)
        gather(k - 1)
    gather(pairs - 1)

    def part_of(layer, h, b):
        return solved_all.at[layer, pl.ds(pl.multiple_of(h * half + b * step_rows, 8), step_rows)]

    def down_copy(b, sem, target):
        ref = part_of(y, core, b)
        return remote(ref, ref, bz_send.at[sem, b], bz_recv.at[b], target)

    def over_copy(b):
        ref = part_of(y, core, b)
        return remote(ref, ref, by_send.at[b], by_recv.at[b], across)

    def over_wait(b):
        ref = part_of(1 - y, core, b)
        remote(ref, ref, by_send.at[b], by_recv.at[b], across).wait_recv()

    def share_copy(turn, b):
        ref = part_of(layer_at(turn), core, b)
        return remote(ref, ref, bs_send.at[turn, b], bs_recv.at[turn, b], sibling)

    def share_wait(turn, b):
        ref = part_of(layer_at(turn), 1 - core, b)
        remote(ref, ref, bs_send.at[turn, b], bs_recv.at[turn, b], sibling).wait_recv()

    @pl.when(is_root)
    def _():
        diagonal = jnp.zeros((TILE, TILE), F32)
        for i in range(strips):
            diagonal = diagonal + corner[i] * eye
        trace = jnp.sum(jnp.sum(diagonal, axis=0, keepdims=True), axis=1, keepdims=True)
        damping = trace * (DAMPING / width)
        for i in range(strips):
            lo, hi = i * TILE, (i + 1) * TILE
            block = corner[i] + damping * eye
            sums[0:1, lo:hi] += jnp.sum(jnp.abs(block), axis=0, keepdims=True)
            hess_high[lo:hi, lo:hi], hess_low[lo:hi, lo:hi] = halves(block)
        upper = jnp.max(sums[0:1], axis=1, keepdims=True)
        theta = (upper + damping) / 2.0
        delta = (upper - damping) / 2.0
        sigma = theta / delta

        for j in range(n // 2):
            at = pl.ds(j * depth, depth)
            source = (y * 0 + core) * (n // 2) + j
            waiting = remote(query.at[0], rhs.at[at], q_send.at[0], q_recv.at[j], sibling)

            @pl.when(source != me)
            def _():
                waiting.wait_recv()

            @pl.when(source == me)
            def _():
                pltpu.make_async_copy(query.at[0], rhs.at[at], q_local).wait()

        mine_rows = pl.ds(pl.multiple_of(core * half, 8), half)
        solved_all[y, mine_rows] = jnp.zeros((half, width), F32)
        direction[...] = rhs[...] / theta

        def step(_, rho):
            current = direction[...]
            solved_all[y, mine_rows] = solved_all[y, mine_rows] + current
            stacked[0:half], stacked[half:2 * half] = halves(current)
            dims = ((1,), (0,))
            wide = dot(stacked[0:2 * half], hess_high[...], dims)
            product = wide[:half] + (wide[half:] + dot(stacked[0:half], hess_low[...], dims))
            resid = rhs[...] - product
            rhs[...] = resid
            rho_new = 1.0 / (2.0 * sigma - rho)
            direction[...] = rho_new * rho * current + (2.0 * rho_new / delta) * resid
            return rho_new

        lax.fori_loop(0, ITERS - 1, step, 1.0 / sigma)
        solved_all[y, mine_rows] = solved_all[y, mine_rows] + direction[...]

    def sent(b):
        @pl.when(jnp.logical_and(z <= root, z > 0))
        def _():
            down_copy(b, 0, me - 4).wait_send()

        @pl.when(jnp.logical_and(z >= root, z < chips - 1))
        def _():
            down_copy(b, 1, me + 4).wait_send()

        over_copy(b).wait_send()
        share_copy(1, b).wait_send()

    for b in range(PIECES):
        @pl.when(jnp.logical_not(is_root))
        def _():
            down_copy(b, 0, me).wait_recv()

        if b >= B_WINDOW:
            sent(b - B_WINDOW)

        @pl.when(jnp.logical_and(z <= root, z > 0))
        def _():
            down_copy(b, 0, me - 4).start()

        @pl.when(jnp.logical_and(z >= root, z < chips - 1))
        def _():
            down_copy(b, 1, me + 4).start()

        over_copy(b).start()
        share_copy(1, b).start()
        if b >= 1:
            over_wait(b - 1)
            share_copy(0, b - 1).start()
    scale = 1.0 / width ** 0.5
    block_rows = min(rows, 2 * TILE)
    count = 2 * half
    for turn in (1, 0):
        if turn == 0:
            over_wait(PIECES - 1)
            share_copy(0, PIECES - 1).start()
        for b in range(PIECES):
            share_wait(turn, b)
        layer = layer_at(turn)
        stacked[0:count], stacked[count:2 * count] = halves(solved_all[layer])

        def score(b, _):
            at = pl.ds(pl.multiple_of(b * block_rows, block_rows), block_rows)
            dims = ((1,), (1,))
            wide = dot(stacked[...], high[turn, at], dims)
            value = wide[:count] + (wide[count:] + dot(stacked[0:count], low[turn, at], dims))
            if turn == 1:
                out[:, at] = value
            else:
                out[:, at] = (out[:, at] + value) * scale
            return 0

        lax.fori_loop(0, rows // block_rows, score, 0)

    for layer in range(layers):
        target, src, slot = query_copy(layer)

        @pl.when(target != me)
        def _():
            remote(src, slot, q_send.at[layer], q_recv.at[my_slot], target).wait_send()

    for k in range(pairs):
        for turn in range(2):
            sib_copy(turn, k).wait_send()
        for s in range(SPLIT):
            if k * SPLIT + s >= pairs * SPLIT - WINDOW:
                y_copy(k, s).wait_send()

            @pl.when(z < root)
            def _():
                left_copy(k, s).wait_send()

            @pl.when(z > root)
            def _():
                right_copy(k, s).wait_send()

            @pl.when(is_root)
            def _():
                full_copy(k, s).wait_send()

    for b in range(PIECES - B_WINDOW, PIECES):
        sent(b)
    for b in range(PIECES):
        share_copy(0, b).wait_send()


def shards(n, train_grads, query_grads):
    layers, rows, width = train_grads.shape
    depth = query_grads.shape[1]
    strips = width // TILE
    pairs, span = strips // 2, (strips + 1) * TILE
    share = TILE // 2
    count = n * depth
    half = count // 2
    dma = pltpu.SemaphoreType.DMA
    return pl.pallas_call(
        functools.partial(kernel, n),
        out_shape=jax.ShapeDtypeStruct((count, rows), F32),
        in_specs=[
            pl.BlockSpec(memory_space=pl.ANY),
            pl.BlockSpec(memory_space=pltpu.VMEM),
        ],
        out_specs=pl.BlockSpec(memory_space=pltpu.VMEM),
        scratch_shapes=[
            pltpu.VMEM((layers, rows, width), F32),
            pltpu.VMEM((layers, rows, width), BF16),
            pltpu.VMEM((layers, rows, width), BF16),
            pltpu.VMEM((layers, pairs, TILE, span), F32),
            pltpu.VMEM((layers, pairs, share, span), F32),
            pltpu.VMEM((layers, pairs, share, span), F32),
            pltpu.VMEM((pairs, share, span), F32),
            pltpu.VMEM((pairs, share, span), F32),
            pltpu.VMEM((pairs, share, span), F32),
            pltpu.VMEM((pairs, TILE, span), F32),
            pltpu.VMEM((strips, TILE, TILE), F32),
            pltpu.VMEM((8, width), F32),
            pltpu.VMEM((width, width), BF16),
            pltpu.VMEM((width, width), BF16),
            pltpu.VMEM((layers, count, width), F32),
            pltpu.VMEM((half, width), F32),
            pltpu.VMEM((half, width), F32),
            pltpu.VMEM((2 * count, width), BF16),
            dma((2,)), dma((layers,)), dma((n // 2,)), dma,
            dma((2, pairs)), dma((2, pairs)),
            dma((pairs, SPLIT)), dma((pairs, SPLIT)),
            dma((pairs, SPLIT)), dma((pairs, SPLIT)), dma((pairs, SPLIT)),
            dma((pairs, SPLIT)), dma((pairs, SPLIT)),
            dma((2, PIECES)), dma((PIECES,)), dma((2, PIECES)),
            dma((PIECES,)), dma((PIECES,)), dma((2, PIECES)),
        ],
        compiler_params=pltpu.CompilerParams(
            collective_id=0, has_side_effects=True, vmem_limit_bytes=60 * 1024 * 1024
        ),
    )(train_grads, query_grads)


def solution(mesh):
    in_specs = (P(None, ("parts", "ex"), None), P(None, ("parts", "ex"), None))
    out_specs = P(None, ("parts", "ex"))
    return jax.shard_map(
        functools.partial(shards, mesh.shape["ex"]),
        mesh=mesh, in_specs=in_specs, out_specs=out_specs, check_vma=False,
    )
```
